512 devices in a mesh: row: 32 (over z_lo, x, core), col: 16 (over z_hi, y).
Axes of the slice: x: 4, y: 4, z: 16 (z_hi: 4, z_lo: 4; z = z_hi * 4 + z_lo), core: 2. Of those that a mesh axis runs over, the one named last changes fastest.
Arguments:
- vectors: bfloat16 [8, 262144], P(None, ('row', 'col')), may hold values from -6 to 6
- block_count: int32 [32, 16], P('row', 'col'), may hold values from 32 to 64, as said below
- block_index: int32 [32, 16, 2, 64], P('row', 'col'), may hold values from 0 to 63, as said below
- blocks: bfloat16 [32, 16, 64, 128, 128], P('row', 'col'), may hold values from -0.0625 to 0.0625
Outputs:
- applied: float32 [8, 262144], P(None, ('row', 'col'))
The draws below stay inside these ranges and needn't reach their ends.
Inputs may be any that keep to these rules, and one draw needn't show every extreme that they name: `block_count`: some grid place has exactly 64 live slots. `block_index`: at grid column 0 each slot's block row is at most its block column. Slots beyond the live count hold indices too.
All inputs are finite; a program needn't handle non-finite values.
Results may differ from the reference program's by a relative error of at most 0.0003.
Values may be sent and summed in bfloat16 or wider, within the bound.
No kernel may reach another device: no remote copies, remote signals or barrier semaphores. Data moves between devices by JAX's collectives and lax.ppermute only.
A program may use at most 64 MiB of HBM per device.

```python
import jax
import jax.numpy as jnp
from jax import lax

NV = 8
BS = 128
SEGB = 64
MAXB = 64
DIM = 262144
N_ROW = 32
N_COL = 16


def draw_block_index(key, part):
    key = jax.random.fold_in(key, 11)
    first_key, second_key = jax.random.split(key)
    first = jax.random.randint(first_key, (N_ROW, N_COL, MAXB), 0, SEGB, dtype=jnp.int32)
    second = jax.random.randint(second_key, (N_ROW, N_COL, MAXB), 0, SEGB, dtype=jnp.int32)
    on_first = (jnp.arange(N_COL, dtype=jnp.int32) == 0)[None, :, None]
    rows_pick = jnp.where(on_first, jnp.minimum(first, second), first)
    cols_pick = jnp.where(on_first, jnp.maximum(first, second), second)
    return jnp.stack([rows_pick, cols_pick], axis=2)


def draw_block_count(key, part):
    key = jax.random.fold_in(key, 12)
    count_key, spot_key = jax.random.split(key)
    counts = jax.random.randint(count_key, (N_ROW * N_COL,), MAXB // 2, MAXB + 1, dtype=jnp.int32)
    spot = jax.random.randint(spot_key, (), 0, N_ROW * N_COL, dtype=jnp.int32)
    counts = jnp.where(jnp.arange(N_ROW * N_COL, dtype=jnp.int32) == spot, MAXB, counts)
    return counts.reshape(N_ROW, N_COL)


def levels(own_key, extent, pieces, least, high):
    def one(axis_at, parts):
        heights = jax.random.uniform(jax.random.fold_in(jax.random.fold_in(own_key, 6), axis_at), (parts,), jnp.float32, least / len(pieces), high / len(pieces))
        return jnp.repeat(jnp.exp(heights), extent[axis_at] // parts).reshape((-1,) + (1,) * (len(extent) - axis_at - 1))

    level = one(*pieces[0])
    for cut in pieces[1:]:
        level = level * one(*cut)
    return level


def noise(own_key, dims, spread, limit, pieces=(), kind=jnp.bfloat16):
    entries = jax.random.normal(own_key, dims, jnp.float32) * spread
    if len(pieces) > 0:
        entries = levels(own_key, dims, pieces, -0.22, 0.18) * entries
    return jnp.clip(entries, min=-limit, max=limit).astype(kind)


def setup_inputs(seed: int = 0) -> dict:
    seeds = jax.random.split(jax.random.key(seed), 5)
    vectors = noise(seeds[0], (NV, DIM), 1.0, 6.0, ((1, 512),))
    block_count = draw_block_count(jax.random.fold_in(seeds[4], 71), 0)
    block_index = draw_block_index(jax.random.fold_in(seeds[4], 71), 0)
    blocks = noise(seeds[3], (N_ROW, N_COL, MAXB, BS, BS), (BS * N_COL * MAXB // SEGB * 4) ** -0.5, 0.0625, ((0, 32), (1, 16)))
    return {"vectors": vectors, "block_count": block_count, "block_index": block_index, "blocks": blocks}


def reference(vectors, block_count, block_index, blocks):
    total_blocks = N_ROW * SEGB
    split = vectors.reshape(NV, total_blocks, BS).astype(jnp.float32)
    col_ids = jnp.arange(N_COL, dtype=jnp.int32)
    slot_ids = jnp.arange(MAXB, dtype=jnp.int32)

    def row_pass(summed, row_id):
        indices = block_index[row_id].astype(jnp.int32)
        partner = (row_id + col_ids) % N_ROW
        rows_at = (row_id * SEGB + indices[:, 0, :]).astype(jnp.int32)
        cols_at = (partner[:, None] * SEGB + indices[:, 1, :]).astype(jnp.int32)
        active = slot_ids[None, :] < block_count[row_id][:, None]
        mirror = active & (rows_at != cols_at)
        matrices = blocks[row_id].astype(jnp.float32)
        far_vec = split[:, cols_at.reshape(-1)].reshape(NV, N_COL, MAXB, BS)
        near_vec = split[:, rows_at.reshape(-1)].reshape(NV, N_COL, MAXB, BS)
        forward = jnp.einsum("cmij,vcmj->vcmi", matrices, far_vec)
        forward = forward * active[None, :, :, None].astype(jnp.float32)
        backward = jnp.einsum("cmij,vcmi->vcmj", matrices, near_vec)
        backward = backward * mirror[None, :, :, None].astype(jnp.float32)
        summed = summed.at[:, rows_at.reshape(-1)].add(forward.reshape(NV, N_COL * MAXB, BS))
        summed = summed.at[:, cols_at.reshape(-1)].add(backward.reshape(NV, N_COL * MAXB, BS))
        return summed, None

    start = jnp.zeros((NV, total_blocks, BS), jnp.float32)
    summed, _ = lax.scan(row_pass, start, jnp.arange(N_ROW, dtype=jnp.int32))
    return summed.reshape(NV, total_blocks * BS)
```

```python
import jax
import jax.numpy as jnp
from jax import lax
from jax.experimental import pallas as pl
from jax.experimental.pallas import tpu as pltpu
from jax.sharding import PartitionSpec as P

PLACES = ("row", "col")


def joint_pairs(to_second):
    rows = lax.axis_size("row")
    cols = lax.axis_size("col")
    pairs = []
    for r in range(rows):
        for c in range(cols):
            first, second = r * cols + c, ((r + c) % rows) * cols + c
            pairs.append((first, second) if to_second else (second, first))
    return pairs


def mirrored_kernel(count_ref, index_ref, near_ref, blocks_ref, out_ref):
    off_first = lax.axis_index("col") != 0
    out_ref[...] = jnp.zeros_like(out_ref)
    live = count_ref[0, 0]
    for m in range(blocks_ref.shape[2]):
        first = index_ref[0, 0, 0, m]
        second = index_ref[0, 0, 1, m]
        keep = (m < live) & (off_first | (first != second))
        product = lax.dot_general(
            near_ref[first], blocks_ref[0, 0, m], (((1,), (0,)), ((), ())), preferred_element_type=jnp.float32
        )
        out_ref[second] = out_ref[second] + jnp.where(keep, product, 0.0)


def direct_kernel(count_ref, index_ref, far_ref, blocks_ref, out_ref):
    out_ref[...] = jnp.zeros_like(out_ref)
    live = count_ref[0, 0]
    for m in range(blocks_ref.shape[2]):
        first = index_ref[0, 0, 0, m]
        second = index_ref[0, 0, 1, m]
        product = lax.dot_general(
            far_ref[second], blocks_ref[0, 0, m], (((1,), (1,)), ((), ())), preferred_element_type=jnp.float32
        )
        out_ref[first] = out_ref[first] + jnp.where(m < live, product, 0.0)


def apply_slots(kernel, count, index, segment, blocks):
    smem = pl.BlockSpec(memory_space=pltpu.SMEM)
    vmem = pl.BlockSpec(memory_space=pltpu.VMEM)
    flops = 2 * segment.shape[1] * blocks.size
    return pl.pallas_call(
        kernel,
        out_shape=jax.ShapeDtypeStruct(segment.shape, jnp.float32),
        in_specs=[smem, smem, vmem, vmem],
        out_specs=vmem,
        compiler_params=pltpu.CompilerParams(vmem_limit_bytes=16 * 1024 * 1024),
        cost_estimate=pl.CostEstimate(flops=flops, bytes_accessed=2 * blocks.size, transcendentals=0),
    )(count, index, segment, blocks)


def per_device(vectors, block_count, block_index, blocks):
    cols = lax.axis_size("col")
    size = blocks.shape[-1]
    nvec, width = vectors.shape
    own = vectors.reshape(nvec, width // size, size).transpose(1, 0, 2)
    near = lax.all_to_all(jnp.tile(own, (cols, 1, 1)), "col", 0, 0, tiled=True)
    far = lax.ppermute(near, PLACES, joint_pairs(False))
    mirrored = apply_slots(mirrored_kernel, block_count, block_index, near, blocks)
    arrived = lax.ppermute(mirrored, PLACES, joint_pairs(True))
    direct = apply_slots(direct_kernel, block_count, block_index, far, blocks)
    shares = lax.all_to_all(direct + arrived, "col", 0, 0, tiled=True)
    total = shares.reshape(cols, width // size, nvec, size).sum(0)
    return total.transpose(1, 0, 2).reshape(nvec, width)


def solution(mesh):
    return jax.shard_map(
        per_device,
        mesh=mesh,
        in_specs=(
            P(None, ("row", "col")),
            P("row", "col"),
            P("row", "col", None, None),
            P("row", "col", None, None, None),
        ),
        out_specs=P(None, ("row", "col")),
        check_vma=False,
    )
```

```python
import functools

import jax
import jax.numpy as jnp
from jax import lax
from jax.experimental import pallas as pl
from jax.experimental.pallas import tpu as pltpu
from jax.sharding import PartitionSpec as P

PLACES = ("row", "col")
TOP = 32767.0
STEPS = 16.0
LEAST = 1e-33


def joint_pairs(to_second):
    rows = lax.axis_size("row")
    cols = lax.axis_size("col")
    pairs = []
    for r in range(rows):
        for c in range(cols):
            first, second = r * cols + c, ((r + c) % rows) * cols + c
            pairs.append((first, second) if to_second else (second, first))
    return pairs


def encode(values, out_ref, chunk):
    peak = functools.reduce(jnp.maximum, [jnp.abs(v) for v in values])
    peak = jnp.maximum(jnp.max(peak, axis=-1, keepdims=True), LEAST)
    power = jnp.ceil(jnp.log2(peak / TOP) * STEPS)
    power = jnp.broadcast_to(power, values[0].shape)
    up = jnp.exp2(power * (-1.0 / STEPS))
    for b, v in enumerate(values):
        code = jnp.clip(jnp.round(v * up), -TOP, TOP)
        out_ref[chunk, b] = code.astype(jnp.int32).astype(jnp.int16)
    out_ref[chunk, len(values)] = power.astype(jnp.int32).astype(jnp.int16)


def decode(in_ref, chunk):
    last = in_ref.shape[1] - 1

    def number(b):
        return in_ref[chunk, b].astype(jnp.int32).astype(jnp.float32)

    down = jnp.exp2(number(last) * (1.0 / STEPS))
    return [number(b) * down for b in range(last)]


def spread_kernel(own_ref, out_ref):
    for n in range(out_ref.shape[0]):
        out_ref[n] = own_ref[...]


def mirrored_kernel(count_ref, index_ref, near_ref, blocks_ref, out_ref, sum_ref):
    off_first = lax.axis_index("col") != 0
    sum_ref[...] = jnp.zeros_like(sum_ref)
    live = count_ref[0, 0]
    for m in range(blocks_ref.shape[2]):
        first = index_ref[0, 0, 0, m]
        second = index_ref[0, 0, 1, m]
        keep = (m < live) & (off_first | (first != second))
        product = lax.dot_general(
            near_ref[first], blocks_ref[0, 0, m], (((1,), (0,)), ((), ())), preferred_element_type=jnp.float32
        )
        sum_ref[second] = sum_ref[second] + jnp.where(keep, product, 0.0)
    chunks, each = out_ref.shape[0], out_ref.shape[1] - 1
    for n in range(chunks):
        encode([sum_ref[n * each + b] for b in range(each)], out_ref, n)


def direct_kernel(count_ref, index_ref, far_ref, blocks_ref, out_ref):
    out_ref[...] = jnp.zeros_like(out_ref)
    live = count_ref[0, 0]
    for m in range(blocks_ref.shape[2]):
        first = index_ref[0, 0, 0, m]
        second = index_ref[0, 0, 1, m]
        product = lax.dot_general(
            far_ref[second], blocks_ref[0, 0, m], (((1,), (1,)), ((), ())), preferred_element_type=jnp.float32
        )
        out_ref[first] = out_ref[first] + jnp.where(m < live, product, 0.0)


def join_kernel(direct_ref, arrived_ref, out_ref):
    chunks, each = out_ref.shape[0], out_ref.shape[1] - 1
    for n in range(chunks):
        arrived = decode(arrived_ref, n)
        encode([direct_ref[n * each + b] + arrived[b] for b in range(each)], out_ref, n)


def total_kernel(shares_ref, out_ref):
    chunks = shares_ref.shape[0]
    total = decode(shares_ref, 0)
    for n in range(1, chunks):
        total = [a + b for a, b in zip(total, decode(shares_ref, n))]
    for b, value in enumerate(total):
        out_ref[b] = value


def call(kernel, out_shape, dtype, args, flops, scalars=0, scratch=()):
    smem = pl.BlockSpec(memory_space=pltpu.SMEM)
    vmem = pl.BlockSpec(memory_space=pltpu.VMEM)
    return pl.pallas_call(
        kernel,
        out_shape=jax.ShapeDtypeStruct(out_shape, dtype),
        in_specs=[smem] * scalars + [vmem] * (len(args) - scalars),
        out_specs=vmem,
        scratch_shapes=scratch,
        compiler_params=pltpu.CompilerParams(vmem_limit_bytes=16 * 1024 * 1024),
        cost_estimate=pl.CostEstimate(flops=flops, bytes_accessed=1 << 20, transcendentals=0),
    )(*args)


def per_device(vectors, block_count, block_index, blocks):
    cols = lax.axis_size("col")
    size = blocks.shape[-1]
    nvec, width = vectors.shape
    each = width // size
    work = 2 * nvec * blocks.size
    own = vectors.reshape(nvec, each, size).transpose(1, 0, 2)
    copies = call(spread_kernel, (cols,) + own.shape, own.dtype, (own,), 1000 * work)
    near = lax.all_to_all(copies.reshape(cols * each, nvec, size), "col", 0, 0, tiled=True)
    far = lax.ppermute(near, PLACES, joint_pairs(False))
    coded = (cols, each + 1, nvec, size)
    sums = pltpu.VMEM(near.shape, jnp.float32)
    mirrored = call(mirrored_kernel, coded, jnp.int16, (block_count, block_index, near, blocks), work, 2, [sums])
    arrived = lax.ppermute(mirrored, PLACES, joint_pairs(True))
    direct = call(direct_kernel, near.shape, jnp.float32, (block_count, block_index, far, blocks), 1000 * work, 2)
    shares = call(join_kernel, coded, jnp.int16, (direct, arrived), work)
    shares = lax.all_to_all(shares, "col", 0, 0, tiled=True)
    total = call(total_kernel, own.shape, jnp.float32, (shares,), work)
    return total.transpose(1, 0, 2).reshape(nvec, width)


def solution(mesh):
    return jax.shard_map(
        per_device,
        mesh=mesh,
        in_specs=(
            P(None, ("row", "col")),
            P("row", "col"),
            P("row", "col", None, None),
            P("row", "col", None, None, None),
        ),
        out_specs=P(None, ("row", "col")),
        check_vma=False,
    )
```

```python
import functools

import jax
import jax.numpy as jnp
from jax import lax
from jax.experimental import pallas as pl
from jax.experimental.pallas import tpu as pltpu
from jax.sharding import PartitionSpec as P

PLACES = ("row", "col")
TOP = 32767.0
STEPS = 16.0
LEAST = 1e-33


def joint_pairs(to_second):
    rows = lax.axis_size("row")
    cols = lax.axis_size("col")
    pairs = []
    for r in range(rows):
        for c in range(cols):
            first, second = r * cols + c, ((r + c) % rows) * cols + c
            pairs.append((first, second) if to_second else (second, first))
    return pairs


def encode(values):
    peak = functools.reduce(jnp.maximum, [jnp.abs(v) for v in values])
    peak = jnp.maximum(jnp.max(peak, axis=-1, keepdims=True), LEAST)
    power = jnp.ceil(jnp.log2(peak / TOP) * STEPS)
    power = jnp.broadcast_to(power, values[0].shape)
    up = jnp.exp2(power * (-1.0 / STEPS))
    codes = [jnp.clip(jnp.round(v * up), -TOP, TOP).astype(jnp.int32).astype(jnp.int16) for v in values]
    return codes, power


def number(code):
    return code.astype(jnp.int32).astype(jnp.float32)


def decode(in_ref, chunk):
    last = in_ref.shape[1] - 1
    down = jnp.exp2(number(in_ref[chunk, last]) * (1.0 / STEPS))
    return [number(in_ref[chunk, b]) * down for b in range(last)]


def spread_kernel(own_ref, out_ref):
    for n in range(out_ref.shape[0]):
        out_ref[n] = own_ref[...]


def mirrored_kernel(each, count_ref, index_ref, near_ref, blocks_ref, out_ref, sum_ref):
    off_first = lax.axis_index("col") != 0
    sum_ref[...] = jnp.zeros_like(sum_ref)
    live = count_ref[0, 0]
    for m in range(blocks_ref.shape[2]):
        first = index_ref[0, 0, 0, m]
        second = index_ref[0, 0, 1, m]
        keep = (m < live) & (off_first | (first != second))
        product = lax.dot_general(
            near_ref[first], blocks_ref[0, 0, m], (((1,), (0,)), ((), ())), preferred_element_type=jnp.float32
        )
        sum_ref[second] = sum_ref[second] + jnp.where(keep, product, 0.0)
    chunks = out_ref.shape[0] // each
    lane = lax.broadcasted_iota(jnp.int32, out_ref.shape[1:], 1)
    powers = jnp.zeros(out_ref.shape[1:], jnp.float32)
    for n in range(chunks):
        codes, power = encode([sum_ref[n * each + b] for b in range(each)])
        powers = jnp.where(lane == n, power, powers)
        for b, code in enumerate(codes):
            out_ref[n * each + b] = code
    out_ref[chunks * each] = powers.astype(jnp.int32).astype(jnp.int16)


def direct_kernel(count_ref, index_ref, far_ref, blocks_ref, out_ref):
    out_ref[...] = jnp.zeros_like(out_ref)
    live = count_ref[0, 0]
    for m in range(blocks_ref.shape[2]):
        first = index_ref[0, 0, 0, m]
        second = index_ref[0, 0, 1, m]
        product = lax.dot_general(
            far_ref[second], blocks_ref[0, 0, m], (((1,), (1,)), ((), ())), preferred_element_type=jnp.float32
        )
        out_ref[first] = out_ref[first] + jnp.where(m < live, product, 0.0)


def join_kernel(direct_ref, arrived_ref, out_ref):
    chunks, each = out_ref.shape[0], out_ref.shape[1] - 1
    downs = jnp.exp2(number(arrived_ref[chunks * each]) * (1.0 / STEPS))
    for n in range(chunks):
        down = jnp.broadcast_to(downs[:, n : n + 1], downs.shape)
        sums = [direct_ref[n * each + b] + number(arrived_ref[n * each + b]) * down for b in range(each)]
        codes, power = encode(sums)
        for b, code in enumerate(codes):
            out_ref[n, b] = code
        out_ref[n, each] = power.astype(jnp.int32).astype(jnp.int16)


def total_kernel(shares_ref, out_ref):
    chunks = shares_ref.shape[0]
    total = decode(shares_ref, 0)
    for n in range(1, chunks):
        total = [a + b for a, b in zip(total, decode(shares_ref, n))]
    for b, value in enumerate(total):
        out_ref[b] = value


def call(kernel, out_shape, dtype, args, flops, scalars=0, scratch=()):
    smem = pl.BlockSpec(memory_space=pltpu.SMEM)
    vmem = pl.BlockSpec(memory_space=pltpu.VMEM)
    return pl.pallas_call(
        kernel,
        out_shape=jax.ShapeDtypeStruct(out_shape, dtype),
        in_specs=[smem] * scalars + [vmem] * (len(args) - scalars),
        out_specs=vmem,
        scratch_shapes=scratch,
        compiler_params=pltpu.CompilerParams(vmem_limit_bytes=16 * 1024 * 1024),
        cost_estimate=pl.CostEstimate(flops=flops, bytes_accessed=1 << 20, transcendentals=0),
    )(*args)


def per_device(vectors, block_count, block_index, blocks):
    cols = lax.axis_size("col")
    size = blocks.shape[-1]
    nvec, width = vectors.shape
    each = width // size
    work = 2 * nvec * blocks.size
    own = vectors.reshape(nvec, each, size).transpose(1, 0, 2)
    copies = call(spread_kernel, (cols,) + own.shape, own.dtype, (own,), 1000 * work)
    near = lax.all_to_all(copies.reshape(cols * each, nvec, size), "col", 0, 0, tiled=True)
    far = lax.ppermute(near, PLACES, joint_pairs(False))
    coded = (cols, each + 1, nvec, size)
    sums = pltpu.VMEM(near.shape, jnp.float32)
    lone = (cols * each + 1, nvec, size)
    kernel = functools.partial(mirrored_kernel, each)
    mirrored = call(kernel, lone, jnp.int16, (block_count, block_index, near, blocks), work, 2, [sums])
    arrived = lax.ppermute(mirrored, PLACES, joint_pairs(True))
    direct = call(direct_kernel, near.shape, jnp.float32, (block_count, block_index, far, blocks), 1000 * work, 2)
    shares = call(join_kernel, coded, jnp.int16, (direct, arrived), work)
    shares = lax.all_to_all(shares, "col", 0, 0, tiled=True)
    total = call(total_kernel, own.shape, jnp.float32, (shares,), work)
    return total.transpose(1, 0, 2).reshape(nvec, width)


def solution(mesh):
    return jax.shard_map(
        per_device,
        mesh=mesh,
        in_specs=(
            P(None, ("row", "col")),
            P("row", "col"),
            P("row", "col", None, None),
            P("row", "col", None, None, None),
        ),
        out_specs=P(None, ("row", "col")),
        check_vma=False,
    )
```

```python
import functools

import jax
import jax.numpy as jnp
from jax import lax
from jax.experimental import pallas as pl
from jax.experimental.pallas import tpu as pltpu
from jax.sharding import PartitionSpec as P

PLACES = ("row", "col")
TOP = 32767.0
STEPS = 16.0
LEAST = 1e-33


def joint_pairs(to_second):
    rows = lax.axis_size("row")
    cols = lax.axis_size("col")
    pairs = []
    for r in range(rows):
        for c in range(cols):
            first, second = r * cols + c, ((r + c) % rows) * cols + c
            pairs.append((first, second) if to_second else (second, first))
    return pairs


def encode(values):
    peak = functools.reduce(jnp.maximum, [jnp.abs(v) for v in values])
    peak = jnp.maximum(jnp.max(peak, axis=-1, keepdims=True), LEAST)
    power = jnp.ceil(jnp.log2(peak / TOP) * STEPS)
    power = jnp.broadcast_to(power, values[0].shape)
    up = jnp.exp2(power * (-1.0 / STEPS))
    codes = [jnp.clip(jnp.round(v * up), -TOP, TOP).astype(jnp.int32).astype(jnp.int16) for v in values]
    return codes, power


def number(code):
    return code.astype(jnp.int32).astype(jnp.float32)


def decode(in_ref, chunk):
    last = in_ref.shape[1] - 1
    down = jnp.exp2(number(in_ref[chunk, last]) * (1.0 / STEPS))
    return [number(in_ref[chunk, b]) * down for b in range(last)]


def spread_kernel(own_ref, out_ref):
    for n in range(out_ref.shape[0]):
        out_ref[n] = own_ref[...]


def mirrored_kernel(each, count_ref, index_ref, near_ref, blocks_ref, out_ref, *sum_refs):
    off_first = lax.axis_index("col") != 0
    live = count_ref[0, 0]
    chunks = out_ref.shape[0] // each
    spare = chunks * each
    for sum_ref in sum_refs:
        sum_ref[...] = jnp.zeros_like(sum_ref)
    nvec, size = near_ref.shape[1:]
    nothing = jnp.zeros((nvec, size), near_ref.dtype)
    for m in range(0, blocks_ref.shape[2], 2):
        first = [index_ref[0, 0, 0, m + n] for n in range(2)]
        second = [index_ref[0, 0, 1, m + n] for n in range(2)]
        one, two = near_ref[first[0]], near_ref[first[1]]
        left = jnp.concatenate([jnp.concatenate([one, nothing], 1), jnp.concatenate([nothing, two], 1)], 0)
        right = blocks_ref[0, 0, m : m + 2].reshape(2 * size, size)
        product = lax.dot_general(left, right, (((1,), (0,)), ((), ())), preferred_element_type=jnp.float32)
        for n, sum_ref in enumerate(sum_refs):
            keep = (m + n < live) & (off_first | (first[n] != second[n]))
            goal = jnp.where(keep, second[n], spare)
            sum_ref[goal] = sum_ref[goal] + product[n * nvec : (n + 1) * nvec]
    lane = lax.broadcasted_iota(jnp.int32, out_ref.shape[1:], 1)
    powers = jnp.zeros(out_ref.shape[1:], jnp.float32)
    for n in range(chunks):
        places = range(n * each, (n + 1) * each)
        codes, power = encode([sum_refs[0][b] + sum_refs[1][b] for b in places])
        powers = jnp.where(lane == n, power, powers)
        for b, code in zip(places, codes):
            out_ref[b] = code
    out_ref[spare] = powers.astype(jnp.int32).astype(jnp.int16)


def direct_kernel(count_ref, index_ref, far_ref, blocks_ref, out_ref, *sum_refs):
    live = count_ref[0, 0]
    spare = out_ref.shape[0]
    for sum_ref in sum_refs:
        sum_ref[...] = jnp.zeros_like(sum_ref)
    nvec, size = far_ref.shape[1:]
    for m in range(0, blocks_ref.shape[2], 2):
        left = jnp.concatenate([far_ref[index_ref[0, 0, 1, m + n]] for n in range(2)], 0)
        right = blocks_ref[0, 0, m : m + 2].reshape(2 * size, size)
        product = lax.dot_general(left, right, (((1,), (1,)), ((), ())), preferred_element_type=jnp.float32)
        for n, sum_ref in enumerate(sum_refs):
            goal = jnp.where(m + n < live, index_ref[0, 0, 0, m + n], spare)
            sum_ref[goal] = sum_ref[goal] + product[n * nvec : (n + 1) * nvec, n * size : (n + 1) * size]
    out_ref[...] = sum_refs[0][0:spare] + sum_refs[1][0:spare]


def join_kernel(direct_ref, arrived_ref, out_ref):
    chunks, each = out_ref.shape[0], out_ref.shape[1] - 1
    lane = lax.broadcasted_iota(jnp.int32, arrived_ref.shape[1:], 1)
    downs = jnp.exp2(number(arrived_ref[chunks * each]) * (1.0 / STEPS))
    for n in range(chunks):
        down = jnp.sum(jnp.where(lane == n, downs, 0.0), axis=1, keepdims=True)
        sums = [direct_ref[n * each + b] + number(arrived_ref[n * each + b]) * down for b in range(each)]
        codes, power = encode(sums)
        for b, code in enumerate(codes):
            out_ref[n, b] = code
        out_ref[n, each] = power.astype(jnp.int32).astype(jnp.int16)


def total_kernel(shares_ref, out_ref):
    chunks = shares_ref.shape[0]
    total = decode(shares_ref, 0)
    for n in range(1, chunks):
        total = [a + b for a, b in zip(total, decode(shares_ref, n))]
    for b, value in enumerate(total):
        out_ref[b] = value


def call(kernel, out_shape, dtype, args, flops, scalars=0, scratch=()):
    smem = pl.BlockSpec(memory_space=pltpu.SMEM)
    vmem = pl.BlockSpec(memory_space=pltpu.VMEM)
    return pl.pallas_call(
        kernel,
        out_shape=jax.ShapeDtypeStruct(out_shape, dtype),
        in_specs=[smem] * scalars + [vmem] * (len(args) - scalars),
        out_specs=vmem,
        scratch_shapes=scratch,
        compiler_params=pltpu.CompilerParams(vmem_limit_bytes=16 * 1024 * 1024),
        cost_estimate=pl.CostEstimate(flops=flops, bytes_accessed=1 << 20, transcendentals=0),
    )(*args)


def per_device(vectors, block_count, block_index, blocks):
    cols = lax.axis_size("col")
    size = blocks.shape[-1]
    nvec, width = vectors.shape
    each = width // size
    work = 2 * nvec * blocks.size
    own = vectors.reshape(nvec, each, size).transpose(1, 0, 2)
    copies = call(spread_kernel, (cols,) + own.shape, own.dtype, (own,), 1000 * work)
    near = lax.all_to_all(copies.reshape(cols * each, nvec, size), "col", 0, 0, tiled=True)
    far = lax.ppermute(near, PLACES, joint_pairs(False))
    coded = (cols, each + 1, nvec, size)
    sums = [pltpu.VMEM((cols * each + 1, nvec, size), jnp.float32)] * 2
    lone = (cols * each + 1, nvec, size)
    kernel = functools.partial(mirrored_kernel, each)
    mirrored = call(kernel, lone, jnp.int16, (block_count, block_index, near, blocks), work, 1, sums)
    arrived = lax.ppermute(mirrored, PLACES, joint_pairs(True))
    direct = call(direct_kernel, near.shape, jnp.float32, (block_count, block_index, far, blocks), 1000 * work, 1, sums)
    shares = call(join_kernel, coded, jnp.int16, (direct, arrived), work)
    shares = lax.all_to_all(shares, "col", 0, 0, tiled=True)
    total = call(total_kernel, own.shape, jnp.float32, (shares,), work)
    return total.transpose(1, 0, 2).reshape(nvec, width)


def solution(mesh):
    return jax.shard_map(
        per_device,
        mesh=mesh,
        in_specs=(
            P(None, ("row", "col")),
            P("row", "col"),
            P("row", "col", None, None),
            P("row", "col", None, None, None),
        ),
        out_specs=P(None, ("row", "col")),
        check_vma=False,
    )
```

```python
import functools

import jax
import jax.numpy as jnp
from jax import lax
from jax.experimental import pallas as pl
from jax.experimental.pallas import tpu as pltpu
from jax.sharding import PartitionSpec as P

PLACES = ("row", "col")
TOP = 32767.0
STEPS = 16.0
LEAST = 1e-33
LEAD_IN = 10
LEAD_OUT = 8


def joint_pairs(to_second):
    rows = lax.axis_size("row")
    cols = lax.axis_size("col")
    pairs = []
    for r in range(rows):
        for c in range(cols):
            first, second = r * cols + c, ((r + c) % rows) * cols + c
            pairs.append((first, second) if to_second else (second, first))
    return pairs


def row_groups(lead):
    rows = lax.axis_size("row")
    cols = lax.axis_size("col")
    return [[r * cols + (lead + c) % cols for c in range(cols)] for r in range(rows)]


def encode(values):
    peak = functools.reduce(jnp.maximum, [jnp.abs(v) for v in values])
    peak = jnp.maximum(jnp.max(peak, axis=-1, keepdims=True), LEAST)
    power = jnp.ceil(jnp.log2(peak / TOP) * STEPS)
    power = jnp.broadcast_to(power, values[0].shape)
    up = jnp.exp2(power * (-1.0 / STEPS))
    codes = [jnp.clip(jnp.round(v * up), -TOP, TOP).astype(jnp.int32).astype(jnp.int16) for v in values]
    return codes, power


def number(code):
    return code.astype(jnp.int32).astype(jnp.float32)


def decode(in_ref, chunk):
    last = in_ref.shape[1] - 1
    down = jnp.exp2(number(in_ref[chunk, last]) * (1.0 / STEPS))
    return [number(in_ref[chunk, b]) * down for b in range(last)]


def spread_kernel(own_ref, out_ref):
    for n in range(out_ref.shape[0]):
        out_ref[n] = own_ref[...]


def mirrored_kernel(each, count_ref, index_ref, near_ref, blocks_ref, out_ref, *sum_refs):
    off_first = lax.axis_index("col") != 0
    live = count_ref[0, 0]
    chunks = out_ref.shape[0] // each
    spare = chunks * each
    turn = spare - LEAD_IN * each
    for sum_ref in sum_refs:
        sum_ref[...] = jnp.zeros_like(sum_ref)
    nvec, size = near_ref.shape[1:]
    nothing = jnp.zeros((nvec, size), near_ref.dtype)
    for m in range(0, blocks_ref.shape[2], 2):
        first = [index_ref[0, 0, 0, m + n] for n in range(2)]
        second = [index_ref[0, 0, 1, m + n] for n in range(2)]
        one, two = [near_ref[(f + turn) % spare] for f in first]
        left = jnp.concatenate([jnp.concatenate([one, nothing], 1), jnp.concatenate([nothing, two], 1)], 0)
        right = blocks_ref[0, 0, m : m + 2].reshape(2 * size, size)
        product = lax.dot_general(left, right, (((1,), (0,)), ((), ())), preferred_element_type=jnp.float32)
        for n, sum_ref in enumerate(sum_refs):
            keep = (m + n < live) & (off_first | (first[n] != second[n]))
            goal = jnp.where(keep, second[n], spare)
            sum_ref[goal] = sum_ref[goal] + product[n * nvec : (n + 1) * nvec]
    lane = lax.broadcasted_iota(jnp.int32, out_ref.shape[1:], 1)
    powers = jnp.zeros(out_ref.shape[1:], jnp.float32)
    for n in range(chunks):
        places = range(n * each, (n + 1) * each)
        codes, power = encode([sum_refs[0][b] + sum_refs[1][b] for b in places])
        powers = jnp.where(lane == n, power, powers)
        for b, code in zip(places, codes):
            out_ref[b] = code
    out_ref[spare] = powers.astype(jnp.int32).astype(jnp.int16)


def direct_kernel(each, count_ref, index_ref, far_ref, blocks_ref, out_ref, *sum_refs):
    live = count_ref[0, 0]
    spare = out_ref.shape[0]
    turn = spare - LEAD_IN * each
    for sum_ref in sum_refs:
        sum_ref[...] = jnp.zeros_like(sum_ref)
    nvec, size = far_ref.shape[1:]
    for m in range(0, blocks_ref.shape[2], 2):
        left = jnp.concatenate([far_ref[(index_ref[0, 0, 1, m + n] + turn) % spare] for n in range(2)], 0)
        right = blocks_ref[0, 0, m : m + 2].reshape(2 * size, size)
        product = lax.dot_general(left, right, (((1,), (1,)), ((), ())), preferred_element_type=jnp.float32)
        for n, sum_ref in enumerate(sum_refs):
            goal = jnp.where(m + n < live, index_ref[0, 0, 0, m + n], spare)
            sum_ref[goal] = sum_ref[goal] + product[n * nvec : (n + 1) * nvec, n * size : (n + 1) * size]
    out_ref[...] = sum_refs[0][0:spare] + sum_refs[1][0:spare]


def join_kernel(direct_ref, arrived_ref, out_ref):
    chunks, each = out_ref.shape[0], out_ref.shape[1] - 1
    lane = lax.broadcasted_iota(jnp.int32, arrived_ref.shape[1:], 1)
    downs = jnp.exp2(number(arrived_ref[chunks * each]) * (1.0 / STEPS))
    for n in range(chunks):
        down = jnp.sum(jnp.where(lane == n, downs, 0.0), axis=1, keepdims=True)
        sums = [direct_ref[n * each + b] + number(arrived_ref[n * each + b]) * down for b in range(each)]
        codes, power = encode(sums)
        place = (n - LEAD_OUT) % chunks
        for b, code in enumerate(codes):
            out_ref[place, b] = code
        out_ref[place, each] = power.astype(jnp.int32).astype(jnp.int16)


def total_kernel(shares_ref, out_ref):
    chunks = shares_ref.shape[0]
    total = decode(shares_ref, 0)
    for n in range(1, chunks):
        total = [a + b for a, b in zip(total, decode(shares_ref, n))]
    for b, value in enumerate(total):
        out_ref[b] = value


def call(kernel, out_shape, dtype, args, flops, scalars=0, scratch=()):
    smem = pl.BlockSpec(memory_space=pltpu.SMEM)
    vmem = pl.BlockSpec(memory_space=pltpu.VMEM)
    return pl.pallas_call(
        kernel,
        out_shape=jax.ShapeDtypeStruct(out_shape, dtype),
        in_specs=[smem] * scalars + [vmem] * (len(args) - scalars),
        out_specs=vmem,
        scratch_shapes=scratch,
        compiler_params=pltpu.CompilerParams(vmem_limit_bytes=16 * 1024 * 1024),
        cost_estimate=pl.CostEstimate(flops=flops, bytes_accessed=1 << 20, transcendentals=0),
    )(*args)


def per_device(vectors, block_count, block_index, blocks):
    cols = lax.axis_size("col")
    size = blocks.shape[-1]
    nvec, width = vectors.shape
    each = width // size
    work = 2 * nvec * blocks.size
    own = vectors.reshape(nvec, each, size).transpose(1, 0, 2)
    copies = call(spread_kernel, (cols,) + own.shape, own.dtype, (own,), 1000 * work)
    copies = copies.reshape(cols * each, nvec, size)
    near = lax.all_to_all(copies, PLACES, 0, 0, axis_index_groups=row_groups(LEAD_IN), tiled=True)
    far = lax.ppermute(near, PLACES, joint_pairs(False))
    coded = (cols, each + 1, nvec, size)
    sums = [pltpu.VMEM((cols * each + 1, nvec, size), jnp.float32)] * 2
    lone = (cols * each + 1, nvec, size)
    kernel = functools.partial(mirrored_kernel, each)
    mirrored = call(kernel, lone, jnp.int16, (block_count, block_index, near, blocks), work, 1, sums)
    arrived = lax.ppermute(mirrored, PLACES, joint_pairs(True))
    kernel = functools.partial(direct_kernel, each)
    direct = call(kernel, near.shape, jnp.float32, (block_count, block_index, far, blocks), 1000 * work, 1, sums)
    shares = call(join_kernel, coded, jnp.int16, (direct, arrived), work)
    shares = lax.all_to_all(shares, PLACES, 0, 0, axis_index_groups=row_groups(LEAD_OUT), tiled=True)
    total = call(total_kernel, own.shape, jnp.float32, (shares,), work)
    return total.transpose(1, 0, 2).reshape(nvec, width)


def solution(mesh):
    return jax.shard_map(
        per_device,
        mesh=mesh,
        in_specs=(
            P(None, ("row", "col")),
            P("row", "col"),
            P("row", "col", None, None),
            P("row", "col", None, None, None),
        ),
        out_specs=P(None, ("row", "col")),
        check_vma=False,
    )
```

```python
import functools

import jax
import jax.numpy as jnp
from jax import lax
from jax.experimental import pallas as pl
from jax.experimental.pallas import tpu as pltpu
from jax.sharding import PartitionSpec as P

PLACES = ("row", "col")
TOP = 32767.0
STEPS = 16.0
LEAST = 1e-33
LEAD_IN = 9
LEAD_OUT = 10


def joint_pairs(to_second):
    rows = lax.axis_size("row")
    cols = lax.axis_size("col")
    pairs = []
    for r in range(rows):
        for c in range(cols):
            first, second = r * cols + c, ((r + c) % rows) * cols + c
            pairs.append((first, second) if to_second else (second, first))
    return pairs


def row_groups(lead):
    rows = lax.axis_size("row")
    cols = lax.axis_size("col")
    return [[r * cols + (lead + c) % cols for c in range(cols)] for r in range(rows)]


def encode(values):
    peak = functools.reduce(jnp.maximum, [jnp.abs(v) for v in values])
    peak = jnp.maximum(jnp.max(peak, axis=-1, keepdims=True), LEAST)
    power = jnp.ceil(jnp.log2(peak / TOP) * STEPS)
    power = jnp.broadcast_to(power, values[0].shape)
    up = jnp.exp2(power * (-1.0 / STEPS))
    codes = [jnp.clip(jnp.round(v * up), -TOP, TOP).astype(jnp.int32).astype(jnp.int16) for v in values]
    return codes, power


def number(code):
    return code.astype(jnp.int32).astype(jnp.float32)


def decode(in_ref, chunk):
    last = in_ref.shape[1] - 1
    down = jnp.exp2(number(in_ref[chunk, last]) * (1.0 / STEPS))
    return [number(in_ref[chunk, b]) * down for b in range(last)]


def spread_kernel(own_ref, out_ref):
    for n in range(out_ref.shape[0]):
        out_ref[n] = own_ref[...]


def mirrored_kernel(each, count_ref, index_ref, near_ref, blocks_ref, out_ref, *sum_refs):
    off_first = lax.axis_index("col") != 0
    live = count_ref[0, 0]
    chunks = out_ref.shape[0] // each
    spare = chunks * each
    turn = spare - LEAD_IN * each
    for sum_ref in sum_refs:
        sum_ref[...] = jnp.zeros_like(sum_ref)
    nvec, size = near_ref.shape[1:]
    nothing = jnp.zeros((nvec, size), near_ref.dtype)
    for m in range(0, blocks_ref.shape[2], 2):
        first = [index_ref[0, 0, 0, m + n] for n in range(2)]
        second = [index_ref[0, 0, 1, m + n] for n in range(2)]
        one, two = [near_ref[(f + turn) % spare] for f in first]
        left = jnp.concatenate([jnp.concatenate([one, nothing], 1), jnp.concatenate([nothing, two], 1)], 0)
        right = blocks_ref[0, 0, m : m + 2].reshape(2 * size, size)
        product = lax.dot_general(left, right, (((1,), (0,)), ((), ())), preferred_element_type=jnp.float32)
        for n, sum_ref in enumerate(sum_refs):
            keep = (m + n < live) & (off_first | (first[n] != second[n]))
            goal = jnp.where(keep, second[n], spare)
            sum_ref[goal] = sum_ref[goal] + product[n * nvec : (n + 1) * nvec]
    lane = lax.broadcasted_iota(jnp.int32, out_ref.shape[1:], 1)
    powers = jnp.zeros(out_ref.shape[1:], jnp.float32)
    for n in range(chunks):
        places = range(n * each, (n + 1) * each)
        codes, power = encode([sum_refs[0][b] + sum_refs[1][b] for b in places])
        powers = jnp.where(lane == n, power, powers)
        for b, code in zip(places, codes):
            out_ref[b] = code
    out_ref[spare] = powers.astype(jnp.int32).astype(jnp.int16)


def direct_kernel(each, count_ref, index_ref, far_ref, blocks_ref, out_ref, *sum_refs):
    live = count_ref[0, 0]
    spare = out_ref.shape[0]
    turn = spare - LEAD_IN * each
    for sum_ref in sum_refs:
        sum_ref[...] = jnp.zeros_like(sum_ref)
    nvec, size = far_ref.shape[1:]
    for m in range(0, blocks_ref.shape[2], 2):
        left = jnp.concatenate([far_ref[(index_ref[0, 0, 1, m + n] + turn) % spare] for n in range(2)], 0)
        right = blocks_ref[0, 0, m : m + 2].reshape(2 * size, size)
        product = lax.dot_general(left, right, (((1,), (1,)), ((), ())), preferred_element_type=jnp.float32)
        for n, sum_ref in enumerate(sum_refs):
            goal = jnp.where(m + n < live, index_ref[0, 0, 0, m + n], spare)
            sum_ref[goal] = sum_ref[goal] + product[n * nvec : (n + 1) * nvec, n * size : (n + 1) * size]
    out_ref[...] = sum_refs[0][0:spare] + sum_refs[1][0:spare]


def join_kernel(direct_ref, arrived_ref, out_ref):
    chunks, each = out_ref.shape[0], out_ref.shape[1] - 1
    lane = lax.broadcasted_iota(jnp.int32, arrived_ref.shape[1:], 1)
    downs = jnp.exp2(number(arrived_ref[chunks * each]) * (1.0 / STEPS))
    for n in range(chunks):
        down = jnp.sum(jnp.where(lane == n, downs, 0.0), axis=1, keepdims=True)
        sums = [direct_ref[n * each + b] + number(arrived_ref[n * each + b]) * down for b in range(each)]
        codes, power = encode(sums)
        place = (n - LEAD_OUT) % chunks
        for b, code in enumerate(codes):
            out_ref[place, b] = code
        out_ref[place, each] = power.astype(jnp.int32).astype(jnp.int16)


def total_kernel(shares_ref, out_ref):
    chunks = shares_ref.shape[0]
    total = decode(shares_ref, 0)
    for n in range(1, chunks):
        total = [a + b for a, b in zip(total, decode(shares_ref, n))]
    for b, value in enumerate(total):
        out_ref[b] = value


def call(kernel, out_shape, dtype, args, flops, scalars=0, scratch=()):
    smem = pl.BlockSpec(memory_space=pltpu.SMEM)
    vmem = pl.BlockSpec(memory_space=pltpu.VMEM)
    return pl.pallas_call(
        kernel,
        out_shape=jax.ShapeDtypeStruct(out_shape, dtype),
        in_specs=[smem] * scalars + [vmem] * (len(args) - scalars),
        out_specs=vmem,
        scratch_shapes=scratch,
        compiler_params=pltpu.CompilerParams(vmem_limit_bytes=16 * 1024 * 1024),
        cost_estimate=pl.CostEstimate(flops=flops, bytes_accessed=1 << 20, transcendentals=0),
    )(*args)


def per_device(vectors, block_count, block_index, blocks):
    cols = lax.axis_size("col")
    size = blocks.shape[-1]
    nvec, width = vectors.shape
    each = width // size
    work = 2 * nvec * blocks.size
    own = vectors.reshape(nvec, each, size).transpose(1, 0, 2)
    copies = call(spread_kernel, (cols,) + own.shape, own.dtype, (own,), 1000 * work)
    copies = copies.reshape(cols * each, nvec, size)
    near = lax.all_to_all(copies, PLACES, 0, 0, axis_index_groups=row_groups(LEAD_IN), tiled=True)
    far = lax.ppermute(near, PLACES, joint_pairs(False))
    coded = (cols, each + 1, nvec, size)
    sums = [pltpu.VMEM((cols * each + 1, nvec, size), jnp.float32)] * 2
    lone = (cols * each + 1, nvec, size)
    kernel = functools.partial(mirrored_kernel, each)
    mirrored = call(kernel, lone, jnp.int16, (block_count, block_index, near, blocks), work, 1, sums)
    arrived = lax.ppermute(mirrored, PLACES, joint_pairs(True))
    kernel = functools.partial(direct_kernel, each)
    direct = call(kernel, near.shape, jnp.float32, (block_count, block_index, far, blocks), 1000 * work, 1, sums)
    shares = call(join_kernel, coded, jnp.int16, (direct, arrived), work)
    shares = lax.all_to_all(shares, PLACES, 0, 0, axis_index_groups=row_groups(LEAD_OUT), tiled=True)
    total = call(total_kernel, own.shape, jnp.float32, (shares,), work)
    return total.transpose(1, 0, 2).reshape(nvec, width)


def solution(mesh):
    return jax.shard_map(
        per_device,
        mesh=mesh,
        in_specs=(
            P(None, ("row", "col")),
            P("row", "col"),
            P("row", "col", None, None),
            P("row", "col", None, None, None),
        ),
        out_specs=P(None, ("row", "col")),
        check_vma=False,
    )
```

```python
import functools

import jax
import jax.numpy as jnp
from jax import lax
from jax.experimental import pallas as pl
from jax.experimental.pallas import tpu as pltpu
from jax.sharding import PartitionSpec as P

PLACES = ("row", "col")
TOP = 32767.0
STEPS = 16.0
LEAST = 1e-33
LEAD_IN = 8
LEAD_OUT = 10


def joint_pairs(to_second):
    rows = lax.axis_size("row")
    cols = lax.axis_size("col")
    pairs = []
    for r in range(rows):
        for c in range(cols):
            first, second = r * cols + c, ((r + c) % rows) * cols + c
            pairs.append((first, second) if to_second else (second, first))
    return pairs


def row_groups(lead):
    rows = lax.axis_size("row")
    cols = lax.axis_size("col")
    return [[r * cols + (lead + c) % cols for c in range(cols)] for r in range(rows)]


def encode(values):
    peak = functools.reduce(jnp.maximum, [jnp.abs(v) for v in values])
    peak = jnp.maximum(jnp.max(peak, axis=-1, keepdims=True), LEAST)
    power = jnp.ceil(jnp.log2(peak / TOP) * STEPS)
    power = jnp.broadcast_to(power, values[0].shape)
    up = jnp.exp2(power * (-1.0 / STEPS))
    codes = [jnp.clip(jnp.round(v * up), -TOP, TOP).astype(jnp.int32).astype(jnp.int16) for v in values]
    return codes, power


def number(code):
    return code.astype(jnp.int32).astype(jnp.float32)


def decode(in_ref, chunk):
    last = in_ref.shape[1] - 1
    down = jnp.exp2(number(in_ref[chunk, last]) * (1.0 / STEPS))
    return [number(in_ref[chunk, b]) * down for b in range(last)]


def spread_kernel(own_ref, out_ref):
    for n in range(out_ref.shape[0]):
        out_ref[n] = own_ref[...]


def mirrored_kernel(each, count_ref, index_ref, near_ref, blocks_ref, out_ref, *sum_refs):
    off_first = lax.axis_index("col") != 0
    live = count_ref[0, 0]
    chunks = out_ref.shape[0] // each
    spare = chunks * each
    turn = spare - LEAD_IN * each
    for sum_ref in sum_refs:
        sum_ref[...] = jnp.zeros_like(sum_ref)
    nvec, size = near_ref.shape[1:]
    nothing = jnp.zeros((nvec, size), near_ref.dtype)
    for m in range(0, blocks_ref.shape[2], 2):
        first = [index_ref[0, 0, 0, m + n] for n in range(2)]
        second = [index_ref[0, 0, 1, m + n] for n in range(2)]
        one, two = [near_ref[(f + turn) & (spare - 1)] for f in first]
        left = jnp.concatenate([jnp.concatenate([one, nothing], 1), jnp.concatenate([nothing, two], 1)], 0)
        right = blocks_ref[0, 0, m : m + 2].reshape(2 * size, size)
        product = lax.dot_general(left, right, (((1,), (0,)), ((), ())), preferred_element_type=jnp.float32)
        for n, sum_ref in enumerate(sum_refs):
            keep = (m + n < live) & (off_first | (first[n] != second[n]))
            goal = jnp.where(keep, second[n], spare)
            sum_ref[goal] = sum_ref[goal] + product[n * nvec : (n + 1) * nvec]
    lane = lax.broadcasted_iota(jnp.int32, out_ref.shape[1:], 1)
    powers = jnp.zeros(out_ref.shape[1:], jnp.float32)
    for n in range(chunks):
        places = range(n * each, (n + 1) * each)
        codes, power = encode([sum_refs[0][b] + sum_refs[1][b] for b in places])
        powers = jnp.where(lane == n, power, powers)
        for b, code in zip(places, codes):
            out_ref[b] = code
    out_ref[spare] = powers.astype(jnp.int32).astype(jnp.int16)


def direct_kernel(each, count_ref, index_ref, far_ref, blocks_ref, out_ref, *sum_refs):
    live = count_ref[0, 0]
    spare = out_ref.shape[0]
    turn = spare - LEAD_IN * each
    for sum_ref in sum_refs:
        sum_ref[...] = jnp.zeros_like(sum_ref)
    nvec, size = far_ref.shape[1:]
    for m in range(0, blocks_ref.shape[2], 2):
        left = jnp.concatenate([far_ref[(index_ref[0, 0, 1, m + n] + turn) & (spare - 1)] for n in range(2)], 0)
        right = blocks_ref[0, 0, m : m + 2].reshape(2 * size, size)
        product = lax.dot_general(left, right, (((1,), (1,)), ((), ())), preferred_element_type=jnp.float32)
        for n, sum_ref in enumerate(sum_refs):
            goal = jnp.where(m + n < live, index_ref[0, 0, 0, m + n], spare)
            sum_ref[goal] = sum_ref[goal] + product[n * nvec : (n + 1) * nvec, n * size : (n + 1) * size]
    out_ref[...] = sum_refs[0][0:spare] + sum_refs[1][0:spare]


def join_kernel(direct_ref, arrived_ref, out_ref):
    chunks, each = out_ref.shape[0], out_ref.shape[1] - 1
    lane = lax.broadcasted_iota(jnp.int32, arrived_ref.shape[1:], 1)
    downs = jnp.exp2(number(arrived_ref[chunks * each]) * (1.0 / STEPS))
    for n in range(chunks):
        down = jnp.sum(jnp.where(lane == n, downs, 0.0), axis=1, keepdims=True)
        sums = [direct_ref[n * each + b] + number(arrived_ref[n * each + b]) * down for b in range(each)]
        codes, power = encode(sums)
        place = (n - LEAD_OUT) % chunks
        for b, code in enumerate(codes):
            out_ref[place, b] = code
        out_ref[place, each] = power.astype(jnp.int32).astype(jnp.int16)


def total_kernel(shares_ref, out_ref):
    chunks = shares_ref.shape[0]
    total = decode(shares_ref, 0)
    for n in range(1, chunks):
        total = [a + b for a, b in zip(total, decode(shares_ref, n))]
    for b, value in enumerate(total):
        out_ref[b] = value


def call(kernel, out_shape, dtype, args, flops, scalars=0, scratch=()):
    smem = pl.BlockSpec(memory_space=pltpu.SMEM)
    vmem = pl.BlockSpec(memory_space=pltpu.VMEM)
    return pl.pallas_call(
        kernel,
        out_shape=jax.ShapeDtypeStruct(out_shape, dtype),
        in_specs=[smem] * scalars + [vmem] * (len(args) - scalars),
        out_specs=vmem,
        scratch_shapes=scratch,
        compiler_params=pltpu.CompilerParams(vmem_limit_bytes=16 * 1024 * 1024),
        cost_estimate=pl.CostEstimate(flops=flops, bytes_accessed=1 << 20, transcendentals=0),
    )(*args)


def per_device(vectors, block_count, block_index, blocks):
    cols = lax.axis_size("col")
    size = blocks.shape[-1]
    nvec, width = vectors.shape
    each = width // size
    work = 2 * nvec * blocks.size
    own = vectors.reshape(nvec, each, size).transpose(1, 0, 2)
    copies = call(spread_kernel, (cols,) + own.shape, own.dtype, (own,), 1000 * work)
    copies = copies.reshape(cols * each, nvec, size)
    near = lax.all_to_all(copies, PLACES, 0, 0, axis_index_groups=row_groups(LEAD_IN), tiled=True)
    far = lax.ppermute(near, PLACES, joint_pairs(False))
    coded = (cols, each + 1, nvec, size)
    sums = [pltpu.VMEM((cols * each + 1, nvec, size), jnp.float32)] * 2
    lone = (cols * each + 1, nvec, size)
    kernel = functools.partial(mirrored_kernel, each)
    mirrored = call(kernel, lone, jnp.int16, (block_count, block_index, near, blocks), work, 1, sums)
    arrived = lax.ppermute(mirrored, PLACES, joint_pairs(True))
    kernel = functools.partial(direct_kernel, each)
    direct = call(kernel, near.shape, jnp.float32, (block_count, block_index, far, blocks), 1000 * work, 1, sums)
    shares = call(join_kernel, coded, jnp.int16, (direct, arrived), work)
    shares = lax.all_to_all(shares, PLACES, 0, 0, axis_index_groups=row_groups(LEAD_OUT), tiled=True)
    total = call(total_kernel, own.shape, jnp.float32, (shares,), work)
    return total.transpose(1, 0, 2).reshape(nvec, width)


def solution(mesh):
    return jax.shard_map(
        per_device,
        mesh=mesh,
        in_specs=(
            P(None, ("row", "col")),
            P("row", "col"),
            P("row", "col", None, None),
            P("row", "col", None, None, None),
        ),
        out_specs=P(None, ("row", "col")),
        check_vma=False,
    )
```
